32 devices in a mesh: groups: 2 (over x), blk: 16 (over z, y, core).
Axes of the slice: x: 2, y: 2, z: 4, core: 2. Of those that a mesh axis runs over, the one named last changes fastest.
Arguments:
- tokens: int32 [4, 64], P(None, 'groups'), parts along dimension 1, may hold values from 0 to 255
- alpha_start: bfloat16 [64, 262144], P('groups', 'blk'), parts along dimension 0, may hold values from 0.25 to 4, as said below
- beta_in: bfloat16 [64, 262144], P('groups', 'blk'), parts along dimension 0, may hold values from 0.25 to 4, as said below
- emission: bfloat16 [256, 512], replicated, may hold values from 0.0099487305 to 1
- left_factor: bfloat16 [512, 512, 512], P('blk'), may hold values from 1.953125e-10 to 0.05859375, as said below
- right_factor: bfloat16 [512, 512, 512], P('blk'), may hold values from 1.953125e-10 to 0.05859375, as said below
Outputs:
- count_left: bfloat16 [1024, 512, 512], P(('groups', 'blk')), parts along dimension 0
- beta_out: bfloat16 [64, 262144], P('groups', 'blk'), parts along dimension 0
- log_scales: float32 [3, 64], P(None, 'groups'), parts along dimension 1
The draws below stay inside these ranges and needn't reach their ends.
There are 2 independent parts, one for each index of `groups`. The reference program is written for one: setup_inputs(seed, part) draws one part's arguments, and reference() takes and returns one part's arrays. A program takes and returns all parts, laid end to end along the dimension named above; an argument that names none is the same for every part. Nothing has to cross between parts.
Inputs may be any that keep to these rules, and one draw needn't show every extreme that they name: `left_factor`: every entry is positive. `right_factor`: every entry is positive. `alpha_start`: every entry is positive. `beta_in`: every entry is positive.
All inputs are finite; a program needn't handle non-finite values.
Results may differ from the reference program's by a relative error of at most 0.0045.
Values may be sent and summed in bfloat16 or wider, within the bound.
A program may use at most 192 MiB of HBM per device.

```python
import math
import jax
import jax.numpy as jnp

B = 512
V = 256
SEQS = 32
STEPS = 4


def band_shape():
    position = jnp.arange(B, dtype=jnp.float32)
    distance = jnp.abs(position[:, None] - position[None, :])
    distance = jnp.minimum(distance, B - distance)
    return 0.05 + 0.95 * jnp.exp(-jnp.square(distance * 16.0 / B))


def message_field(levels, noise):
    field = jnp.exp(levels + noise)
    field = jnp.clip(field, 0.25, 4.0)
    return field.reshape(SEQS, B * B).astype(jnp.bfloat16)


def draw_left_factor(key, part):
    key = jax.random.fold_in(key, 11)
    gain_key, pair_key, key = jax.random.split(key, 3)
    lead = 1.0 + 2.0 * jnp.arange(B, dtype=jnp.float32)[:, None, None] / (B - 1)
    gains = jnp.exp(jax.random.uniform(gain_key, (B, 1, 1), jnp.float32, -2.0, 2.0))
    pairs = jnp.exp(jax.random.uniform(pair_key, (B, B, 1), jnp.float32, -1.0, 1.0))
    values = jnp.exp(jax.random.uniform(key, (B, B, B), jnp.float32, math.log(0.001), 0.0)) * 0.45 / B
    return (values * lead * gains * pairs * band_shape()[None, :, :]).astype(jnp.bfloat16)


def draw_right_factor(key, part):
    key = jax.random.fold_in(key, 23)
    gain_key, pair_key, key = jax.random.split(key, 3)
    lead = 1.0 + 2.0 * jnp.arange(B, dtype=jnp.float32)[:, None, None] / (B - 1)
    gains = jnp.exp(jax.random.uniform(gain_key, (B, 1, 1), jnp.float32, -2.0, 2.0))
    pairs = jnp.exp(jax.random.uniform(pair_key, (B, 1, B), jnp.float32, -1.0, 1.0))
    values = jnp.exp(jax.random.uniform(key, (B, B, B), jnp.float32, math.log(0.001), 0.0)) * 0.45 / B
    return (values * lead * gains * pairs * band_shape()[None, :, :]).astype(jnp.bfloat16)


def draw_alpha_start(key, part):
    key = jax.random.fold_in(key, 31)
    level_key, noise_key = jax.random.split(key)
    segment_count = 32
    levels = jax.random.uniform(level_key, (SEQS, B, segment_count, 1), jnp.float32, -math.log(4.0), math.log(4.0))
    noise = jax.random.uniform(noise_key, (SEQS, B, segment_count, B // segment_count), jnp.float32, -0.5, 0.5)
    return message_field(levels, noise)


def draw_beta_in(key, part):
    key = jax.random.fold_in(key, 37)
    level_key, noise_key = jax.random.split(key)
    segment_count = 32
    levels = jax.random.uniform(level_key, (SEQS, B, segment_count, 1), jnp.float32, -math.log(4.0), math.log(4.0))
    noise = jax.random.uniform(noise_key, (SEQS, B, segment_count, B // segment_count), jnp.float32, -0.5, 0.5)
    return message_field(levels, noise)


def with_ends(values, rng, least, top_value):
    longest = values.shape.index(max(values.shape))
    spots = []
    for shift in (0, 1):
        where = [jax.random.randint(jax.random.fold_in(rng, axis), (), 0, length) for axis, length in enumerate(values.shape)]
        where[longest] = (where[longest] + shift) % values.shape[longest]
        spots.append(tuple(where))
    return values.at[spots[0]].set(least).at[spots[1]].set(top_value)


def setup_inputs(seed: int = 0, part: int = 0) -> dict:
    keys = jax.random.split(jax.random.key(seed), 7)
    own_keys = jax.random.split(jax.random.fold_in(keys[6], part), 7)
    return {
        "tokens": with_ends(jax.random.randint(own_keys[0], (STEPS, SEQS), 0, V), jax.random.fold_in(own_keys[0], 1), 0, V - 1).astype(jnp.int32),
        "alpha_start": draw_alpha_start(jax.random.fold_in(jax.random.fold_in(keys[6], part), 71), part),
        "beta_in": draw_beta_in(jax.random.fold_in(jax.random.fold_in(keys[6], part), 71), part),
        "emission": jnp.clip(jnp.exp(jax.random.uniform(keys[3], (V, B), jnp.float32, math.log(0.0099487305), math.log(1.0))), 0.0099487305, 1.0).astype(jnp.bfloat16),
        "left_factor": draw_left_factor(jax.random.fold_in(keys[6], 71), part),
        "right_factor": draw_right_factor(jax.random.fold_in(keys[6], 71), part),
    }


def reference(tokens, alpha_start, beta_in, emission, left_factor, right_factor):
    states = B * B
    left = left_factor.astype(jnp.float32)
    right = right_factor.astype(jnp.float32)

    def emission_rows(step):
        return emission[tokens[step]].astype(jnp.float32)[:, None, :]

    forward_msg = alpha_start.reshape(SEQS, B, B)
    forwards = [forward_msg]
    paths = []
    log_rows = []
    for step in range(1, STEPS + 1):
        path_sums = jnp.einsum("nrs,rsp->npr", forward_msg.astype(jnp.float32), right).astype(jnp.bfloat16)
        paths.append(path_sums)
        if step < STEPS:
            ahead = jnp.einsum("npr,prq->npq", path_sums.astype(jnp.float32), left)
            weighted = ahead * emission_rows(step - 1)
            forward_total = jnp.sum(weighted, axis=(1, 2))
            log_rows.append(jnp.log(forward_total / states))
            forward_msg = (states * weighted / forward_total[:, None, None]).astype(jnp.bfloat16)
            forwards.append(forward_msg)

    backward_msg = beta_in.reshape(SEQS, B, B)
    weights = []
    values = []
    for step in range(STEPS, 0, -1):
        emitted = (emission_rows(step - 1) * backward_msg.astype(jnp.float32)).astype(jnp.bfloat16)
        back_sums = jnp.einsum("npq,prq->npr", emitted.astype(jnp.float32), left).astype(jnp.bfloat16)
        prior = jnp.einsum("npr,rsp->nrs", back_sums.astype(jnp.float32), right)
        norm_total = jnp.sum(prior, axis=(1, 2))
        posterior_total = jnp.sum(forwards[step - 1].astype(jnp.float32) * prior, axis=(1, 2))
        weights.append((paths[step - 1].astype(jnp.float32) / posterior_total[:, None, None]).astype(jnp.bfloat16))
        values.append(emitted)
        backward_msg = (states * prior / norm_total[:, None, None]).astype(jnp.bfloat16)

    stacked_weights = jnp.concatenate(weights, axis=0).astype(jnp.float32)
    stacked_values = jnp.concatenate(values, axis=0).astype(jnp.float32)
    tally = jnp.einsum("npr,npq->prq", stacked_weights, stacked_values)
    count_left = (left * tally * (B * states / SEQS)).astype(jnp.bfloat16)
    log_scales = jnp.stack(log_rows, axis=0)
    return count_left, backward_msg.reshape(SEQS, states), log_scales
```

```python
import functools

import jax
import jax.numpy as jnp
from jax import lax
from jax.experimental import pallas as pl
from jax.experimental.pallas import tpu as pltpu
from jax.sharding import PartitionSpec as P

LANES = 128
SUBLANES = 8
MIB = 1 << 20


def dot(x, w, w_dim):
    return lax.dot_general(
        x, w, (((1,), (w_dim,)), ((), ())), preferred_element_type=jnp.float32
    )


def messages_kernel(
    devices,
    window,
    alpha_hbm,
    beta_hbm,
    left_hbm,
    right_hbm,
    rows_ref,
    paths_hbm,
    values_hbm,
    beta_out_hbm,
    totals_ref,
    post_ref,
    mean_ref,
    left,
    right,
    alpha_first,
    alphas,
    beta_flat,
    prior_last_step,
    values,
    paths,
    staged,
    unpacked,
    outbox,
    inbox,
    small_out,
    small_in,
    post_sums,
    left_sem,
    right_sem,
    message_sem,
    out_sem,
    own_sem,
    send_sem,
    recv_sem,
    small_send_sem,
    small_recv_sem,
):
    blocks, size, _ = left.shape
    seqs = alpha_first.shape[0]
    states = size * size
    tiles = size // LANES
    group = LANES // blocks
    steps = window - 1
    chunks = left_sem.shape[0]
    per_chunk = blocks // chunks
    me = lax.axis_index("blk")

    def loop(count, body, start=0, unroll=1):
        def wrapped(i, carry):
            body(i)
            return carry

        lax.fori_loop(start, count, wrapped, 0, unroll=unroll)

    def chunk_copy(hbm, ref, sem, c):
        part = pl.ds(c * per_chunk, per_chunk)
        return pltpu.make_async_copy(hbm.at[part], ref.at[part], sem.at[c])

    alpha_copy = pltpu.make_async_copy(alpha_hbm, alpha_first, message_sem.at[0])
    beta_copy = pltpu.make_async_copy(beta_hbm, beta_flat, message_sem.at[1])
    alpha_copy.start()
    loop(chunks, lambda c: chunk_copy(right_hbm, right, right_sem, c).start())
    beta_copy.start()
    loop(chunks, lambda c: chunk_copy(left_hbm, left, left_sem, c).start())

    barrier = pltpu.get_barrier_semaphore()

    def greet(off):
        pl.semaphore_signal(
            barrier,
            inc=1,
            device_id={"blk": lax.rem(me + off, devices)},
            device_id_type=pl.DeviceIdType.MESH,
        )

    loop(devices, greet, 1)
    pl.semaphore_wait(barrier, devices - 1)

    def block_copy(chain, par, off, landing):
        other = lax.rem(me + off, devices)
        return pltpu.make_async_remote_copy(
            src_ref=outbox.at[chain, pl.ds(pl.multiple_of(other * blocks, blocks), blocks)],
            dst_ref=inbox.at[chain, par, landing(other)],
            send_sem=send_sem.at[chain, off],
            recv_sem=recv_sem.at[chain, par, landing(other)],
            device_id={"blk": other},
            device_id_type=pl.DeviceIdType.MESH,
        )

    def own_copy(chain, par):
        return pltpu.make_async_copy(
            outbox.at[chain, pl.ds(pl.multiple_of(me * blocks, blocks), blocks)],
            inbox.at[chain, par, me],
            own_sem.at[chain],
        )

    def sent(chain, par):
        loop(devices, lambda off: block_copy(chain, par, off, lambda other: me).wait_send(), 1)

    def pack_and_send(chain, par):
        def pack(j):
            lanes = pl.ds(pl.multiple_of(j * LANES, LANES), LANES)
            for k in range(tiles):
                picked = [
                    staged[k, pl.ds(j * group + c, blocks, stride=seqs), :] for c in range(group)
                ]
                turned = jnp.transpose(jnp.concatenate(picked, axis=0))
                outbox[chain, k * LANES : (k + 1) * LANES, lanes] = turned.astype(jnp.bfloat16)

        loop(seqs // group, pack)
        loop(devices, lambda off: block_copy(chain, par, off, lambda other: me).start(), 1)
        own_copy(chain, par).start()

    def receive(chain, par):
        own_copy(chain, par).wait()
        loop(devices, lambda off: block_copy(chain, par, off, lambda other: other).wait_recv(), 1)
        place = lax.broadcasted_iota(jnp.int32, (blocks, LANES), 1) // blocks

        def merge(pieces):
            merged = pieces[0]
            for g in range(1, group):
                merged = jnp.where(place == g, pieces[g], merged)
            return merged

        def unpack(j):
            lanes = pl.ds(pl.multiple_of(j * LANES, LANES), LANES)
            for k in range(tiles):
                came = [
                    inbox[chain, par, k * group + i, :, lanes].astype(jnp.float32)
                    for i in range(group)
                ]
                shifted = []
                for s in range(group):
                    mixed = merge([came[(g + s) % group] for g in range(group)])
                    shifted.append(pltpu.roll(mixed, s * blocks, 1) if s else mixed)
                for c in range(group):
                    unpacked[k, pl.ds(j * group + c, blocks, stride=seqs), :] = merge(
                        [shifted[(i - c) % group] for i in range(group)]
                    )

        loop(seqs // group, unpack)

    def small_copy(kind, slot, off, landing):
        other = lax.rem(me + off, devices)
        return pltpu.make_async_remote_copy(
            src_ref=small_out.at[kind],
            dst_ref=small_in.at[slot, landing(other)],
            send_sem=small_send_sem.at[kind, off],
            recv_sem=small_recv_sem.at[slot, landing(other)],
            device_id={"blk": other},
            device_id_type=pl.DeviceIdType.MESH,
        )

    def small_sent(kind, slot):
        loop(devices, lambda off: small_copy(kind, slot, off, lambda other: me).wait_send(), 1)

    def small_send(kind, slot, columns):
        lane = lax.broadcasted_iota(jnp.int32, (SUBLANES, LANES), 1)
        tile = jnp.zeros((SUBLANES, LANES), jnp.float32)
        for c, column in enumerate(columns):
            for i in range(seqs // SUBLANES):
                part = column[i * SUBLANES : (i + 1) * SUBLANES, :]
                tile = jnp.where(lane == c * (seqs // SUBLANES) + i, part, tile)
        small_out[kind] = tile
        small_in[slot, me] = tile
        loop(devices, lambda off: small_copy(kind, slot, off, lambda other: me).start(), 1)

    def small_receive(kind, slot, count):
        loop(devices, lambda off: small_copy(kind, slot, off, lambda other: other).wait_recv(), 1)
        total = jnp.sum(small_in[slot], axis=0)
        per = seqs // SUBLANES
        return [
            jnp.concatenate(
                [total[:, c * per + i : c * per + i + 1] for i in range(per)], axis=0
            )
            for c in range(count)
        ]

    def flat(b):
        return pl.ds(pl.multiple_of(b * size, size), size)

    def block_rows(b):
        return pl.ds(pl.multiple_of(b * seqs, seqs), seqs)

    def stage(b, result):
        for k in range(tiles):
            staged[k, block_rows(b), :] = result[:, k * LANES : (k + 1) * LANES]

    def arrived(b):
        return jnp.concatenate(
            [unpacked[k, block_rows(b), :] for k in range(tiles)], axis=1
        ).astype(jnp.bfloat16)

    def narrow(wide):
        total = wide[:, :LANES]
        for k in range(1, tiles):
            total = total + wide[:, k * LANES : (k + 1) * LANES]
        return total

    zero = jnp.zeros((seqs, LANES), jnp.float32)

    def column(total):
        return jnp.sum(total, axis=1, keepdims=True)

    alpha_copy.wait()

    def first_path(c):
        chunk_copy(right_hbm, right, right_sem, c).wait()
        loop(
            per_chunk,
            lambda i: stage(
                c * per_chunk + i,
                dot(alpha_first[:, flat(c * per_chunk + i)], right[c * per_chunk + i], 0),
            ),
        )

    loop(chunks, first_path)
    pack_and_send(0, 0)
    even = jnp.full((seqs, 1), states / devices, jnp.float32)
    small_send(0, 0, [even])

    beta_copy.wait()

    def first_back(c):
        chunk_copy(left_hbm, left, left_sem, c).wait()

        def one(i):
            b = c * per_chunk + i
            emitted = rows_ref[steps].astype(jnp.float32) * beta_flat[:, flat(b)].astype(
                jnp.float32
            )
            values[steps, b] = emitted.astype(jnp.bfloat16)
            stage(b, dot(values[steps, b], left[b], 1))

        loop(per_chunk, one)

    loop(chunks, first_back)
    pack_and_send(1, 0)
    small_send(1, 2, [even])

    def values_copy(t):
        return pltpu.make_async_copy(values.at[t], values_hbm.at[:, t], out_sem.at[0, t])

    def paths_copy(t):
        return pltpu.make_async_copy(paths.at[t], paths_hbm.at[:, t], out_sem.at[1, t])

    values_copy(steps).start()

    def keep_mean(ref, index, total):
        mean = total * (1.0 / states)
        ref[index] = jnp.broadcast_to(mean, (seqs, LANES))
        return 1.0 / mean

    def step_body(k):
        par, later = lax.rem(k, 2), lax.rem(k + 1, 2)

        receive(0, par)
        (total,) = small_receive(0, par, 1)
        scale = keep_mean(totals_ref, k, total)

        def forward(b, acc):
            path = arrived(b)
            paths[k, b] = path
            ahead = dot(path, left[b], 0)
            weighted = ahead * (rows_ref[k].astype(jnp.float32) * scale)
            alphas[k, b] = weighted.astype(jnp.bfloat16)
            return acc + narrow(weighted)

        acc = lax.fori_loop(0, blocks, forward, zero, unroll=2)
        small_sent(0, par)
        small_send(0, later, [column(acc)])
        paths_copy(k).start()
        loop(blocks, lambda b: stage(b, dot(alphas[k, b], right[b], 0)), unroll=2)
        sent(0, par)
        pack_and_send(0, later)

        receive(1, par)
        (total,) = small_receive(1, 2 + par, 1)
        scale = keep_mean(mean_ref, steps - k, total)

        def backward(b, accs):
            prior = dot(arrived(b), right[b], 1) * scale
            prior_last_step[lax.min(k, 1), b] = prior.astype(jnp.bfloat16)
            emitted = rows_ref[steps - 1 - k].astype(jnp.float32) * prior
            values[steps - 1 - k, b] = emitted.astype(jnp.bfloat16)
            both = alphas[post_source(k), b].astype(jnp.float32) * prior
            return accs[0] + narrow(prior), accs[1] + narrow(both)

        acc, post = lax.fori_loop(0, blocks, backward, (zero, zero), unroll=2)
        small_sent(1, 2 + par)
        small_send(1, 2 + later, [column(acc)])
        post_sums[steps - k] = post
        values_copy(steps - 1 - k).start()
        loop(
            blocks,
            lambda b: stage(b, dot(values[steps - 1 - k, b], left[b], 1)),
            unroll=2,
        )
        sent(1, par)
        pack_and_send(1, later)

    def post_source(k):
        return lax.min(steps - 1 - k, k)

    loop(steps, step_body)
    par = steps % 2

    for late in range(steps):
        if steps - 1 - late > late:

            def late_post(b, acc):
                both = alphas[steps - 1 - late, b].astype(jnp.float32) * prior_last_step[
                    late, b
                ].astype(jnp.float32)
                return acc + narrow(both)

            post_sums[steps - late] = lax.fori_loop(0, blocks, late_post, zero)

    receive(0, par)
    (total,) = small_receive(0, par, 1)
    keep_mean(totals_ref, steps, total)

    def last_path(b):
        paths[steps, b] = arrived(b)

    loop(blocks, last_path)
    paths_copy(steps).start()

    receive(1, par)
    (total,) = small_receive(1, 2 + par, 1)
    scale = keep_mean(mean_ref, 0, total)

    def last_prior(b, accs):
        prior = dot(arrived(b), right[b], 1) * scale
        stage(b, prior)
        both = alpha_first[:, flat(b)].astype(jnp.float32) * prior
        return accs[0] + narrow(prior), accs[1] + narrow(both)

    acc, post = lax.fori_loop(0, blocks, last_prior, (zero, zero), unroll=2)
    post_sums[0] = post
    small_send(2, 4, [column(acc)] + [column(post_sums[t]) for t in range(window)])
    found = small_receive(2, 4, 1 + window)
    norm = states / found[0]
    for t in range(window):
        post_ref[t] = jnp.broadcast_to(found[1 + t], (seqs, LANES))

    def last_beta(b):
        wide = jnp.concatenate([staged[k, block_rows(b), :] for k in range(tiles)], axis=1)
        beta_flat[:, flat(b)] = (wide * norm).astype(jnp.bfloat16)

    loop(blocks, last_beta)
    result = pltpu.make_async_copy(beta_flat, beta_out_hbm, message_sem.at[0])
    result.start()
    for t in range(window):
        values_copy(t).wait()
        paths_copy(t).wait()
    sent(0, par)
    sent(1, par)
    small_sent(0, par)
    small_sent(1, 2 + par)
    small_sent(2, 4)
    result.wait()


def counts_kernel(factor, post_ref, mean_ref, left_ref, paths_ref, values_ref, count_ref):
    for i in range(left_ref.shape[0]):
        scaled = paths_ref[i].astype(jnp.float32) / post_ref[:, :1] / mean_ref[:, :1]
        tally = lax.dot_general(
            scaled.astype(jnp.bfloat16),
            values_ref[i],
            (((0,), (0,)), ((), ())),
            preferred_element_type=jnp.float32,
        )
        count_ref[i] = (left_ref[i].astype(jnp.float32) * tally * factor).astype(jnp.bfloat16)


def on_device_fused(devices, tokens, alpha_start, beta_in, emission, left_factor, right_factor):
    blocks, size, _ = left_factor.shape
    seqs = alpha_start.shape[0]
    window = tokens.shape[0]
    vocab = emission.shape[0]
    steps = window - 1
    picked = tokens.reshape(-1)[:, None] == lax.broadcasted_iota(
        jnp.int32, (window * seqs, vocab), 1
    )
    rows = jnp.dot(
        picked.astype(jnp.bfloat16), emission, preferred_element_type=jnp.float32
    ).reshape(window, seqs, size)
    any_space = pl.BlockSpec(memory_space=pl.ANY)
    in_vmem = pl.BlockSpec(memory_space=pltpu.VMEM)
    bf16, f32 = jnp.bfloat16, jnp.float32
    tiles = size // LANES
    chunks = 4
    per_step = jax.ShapeDtypeStruct((window, seqs, LANES), f32)
    kept = jax.ShapeDtypeStruct((blocks, window, seqs, size), bf16)
    messages = (blocks, seqs, size)
    turned = (tiles, blocks * seqs, LANES)
    paths, values, beta_out, totals, post, mean = pl.pallas_call(
        functools.partial(messages_kernel, devices, window),
        out_shape=(
            kept,
            kept,
            jax.ShapeDtypeStruct(beta_in.shape, bf16),
            per_step,
            per_step,
            per_step,
        ),
        in_specs=[any_space] * 4 + [in_vmem],
        out_specs=(any_space,) * 3 + (in_vmem,) * 3,
        scratch_shapes=[
            pltpu.VMEM(left_factor.shape, bf16),
            pltpu.VMEM(right_factor.shape, bf16),
            pltpu.VMEM(alpha_start.shape, bf16),
            pltpu.VMEM((steps,) + messages, bf16),
            pltpu.VMEM(beta_in.shape, bf16),
            pltpu.VMEM((2,) + messages, bf16),
            pltpu.VMEM((window,) + messages, bf16),
            pltpu.VMEM((window,) + messages, bf16),
            pltpu.VMEM(turned, f32),
            pltpu.VMEM(turned, f32),
            pltpu.VMEM((2, size, seqs * blocks), bf16),
            pltpu.VMEM((2, 2, devices, blocks, seqs * blocks), bf16),
            pltpu.VMEM((3, SUBLANES, LANES), f32),
            pltpu.VMEM((5, devices, SUBLANES, LANES), f32),
            pltpu.VMEM((window, seqs, LANES), f32),
            pltpu.SemaphoreType.DMA((chunks,)),
            pltpu.SemaphoreType.DMA((chunks,)),
            pltpu.SemaphoreType.DMA((2,)),
            pltpu.SemaphoreType.DMA((2, window)),
            pltpu.SemaphoreType.DMA((2,)),
            pltpu.SemaphoreType.DMA((2, devices)),
            pltpu.SemaphoreType.DMA((2, 2, devices)),
            pltpu.SemaphoreType.DMA((3, devices)),
            pltpu.SemaphoreType.DMA((5, devices)),
        ],
        compiler_params=pltpu.CompilerParams(
            collective_id=0, has_side_effects=True, vmem_limit_bytes=62 * MIB
        ),
    )(alpha_start, beta_in, left_factor, right_factor, rows)
    per_call = 2
    rows_all = window * seqs
    factor = size * (size * size / seqs)
    scale_spec = pl.BlockSpec((rows_all, LANES), lambda b: (0, 0))
    factor_spec = pl.BlockSpec((per_call, size, size), lambda b: (b, 0, 0))
    kept_spec = pl.BlockSpec((per_call, rows_all, size), lambda b: (b, 0, 0))
    count_left = pl.pallas_call(
        functools.partial(counts_kernel, factor),
        grid=(blocks // per_call,),
        out_shape=jax.ShapeDtypeStruct(left_factor.shape, bf16),
        in_specs=[scale_spec, scale_spec, factor_spec, kept_spec, kept_spec],
        out_specs=factor_spec,
        compiler_params=pltpu.CompilerParams(vmem_limit_bytes=32 * MIB),
    )(
        post.reshape(rows_all, LANES),
        mean.reshape(rows_all, LANES),
        left_factor,
        paths.reshape(blocks, rows_all, size),
        values.reshape(blocks, rows_all, size),
    )
    log_scales = jnp.log(totals[1:, :, 0])
    return count_left, beta_out, log_scales


def fused_fits(seqs, blocks, size):
    if blocks % 16 or LANES % blocks or size % LANES or seqs % 16:
        return False
    return seqs % (LANES // blocks) == 0


def on_device(tokens, alpha_start, beta_in, emission, left_factor, right_factor):
    blocks_dev, block_size, _ = left_factor.shape
    seq_count = alpha_start.shape[0]
    window = tokens.shape[0]
    vocab_size = emission.shape[0]
    states = block_size * block_size

    def emission_rows(step):
        picked = tokens[step][:, None] == lax.broadcasted_iota(
            jnp.int32, (seq_count, vocab_size), 1
        )
        rows = jnp.dot(picked.astype(jnp.bfloat16), emission, preferred_element_type=jnp.float32)
        return rows[None, :, :]

    def path_sums(message):
        return jnp.einsum(
            "rns,rsp->rnp", message, right_factor, preferred_element_type=jnp.float32
        ).astype(jnp.bfloat16)

    forward_msg = jnp.transpose(alpha_start.reshape(seq_count, blocks_dev, block_size), (1, 0, 2))
    forwards = [forward_msg]
    received = []
    log_rows = []
    for step in range(1, window):
        arrived = lax.all_to_all(
            path_sums(forward_msg), "blk", split_axis=2, concat_axis=0, tiled=True
        )
        turned_paths = jnp.transpose(arrived, (2, 1, 0))
        received.append(turned_paths)
        ahead = jnp.einsum(
            "pnr,prq->pnq", turned_paths, left_factor, preferred_element_type=jnp.float32
        )
        weighted = ahead * emission_rows(step - 1)
        forward_total = lax.psum(jnp.sum(weighted, axis=(0, 2)), "blk")
        log_rows.append(jnp.log(forward_total / states))
        forward_msg = (states * weighted / forward_total[None, :, None]).astype(jnp.bfloat16)
        forwards.append(forward_msg)
    last_send = path_sums(forward_msg)
    received.append(
        jnp.transpose(
            lax.all_to_all(last_send, "blk", split_axis=2, concat_axis=0, tiled=True), (2, 1, 0)
        )
    )
    backward_msg = jnp.transpose(beta_in.reshape(seq_count, blocks_dev, block_size), (1, 0, 2))
    weights = []
    values = []
    for step in range(window, 0, -1):
        emitted = (emission_rows(step - 1) * backward_msg).astype(jnp.bfloat16)
        back_sums = jnp.einsum(
            "pnq,prq->pnr", emitted, left_factor, preferred_element_type=jnp.float32
        ).astype(jnp.bfloat16)
        if step == window:
            turned = lax.all_to_all(back_sums, "blk", split_axis=2, concat_axis=0, tiled=True)
        else:
            turned = lax.all_to_all(back_sums, "blk", split_axis=2, concat_axis=0, tiled=True)
        turned_back = jnp.transpose(turned, (2, 1, 0))
        prior = jnp.einsum(
            "rnp,rsp->rns", turned_back, right_factor, preferred_element_type=jnp.float32
        )
        norm_total, posterior_total = lax.psum(
            (jnp.sum(prior, axis=(0, 2)), jnp.sum(forwards[step - 1] * prior, axis=(0, 2))), "blk"
        )
        weights.append(
            (received[step - 1].astype(jnp.float32) / posterior_total[None, :, None]).astype(
                jnp.bfloat16
            )
        )
        values.append(emitted)
        backward_msg = (states * prior / norm_total[None, :, None]).astype(jnp.bfloat16)
    stacked_weights = jnp.concatenate(weights, axis=1)
    stacked_values = jnp.concatenate(values, axis=1)
    tally = jnp.einsum(
        "pnr,pnq->prq", stacked_weights, stacked_values, preferred_element_type=jnp.float32
    )
    count_left = (left_factor * tally * (block_size * states / seq_count)).astype(jnp.bfloat16)
    log_scales = jnp.stack(log_rows, axis=0)
    beta_out = jnp.transpose(backward_msg, (1, 0, 2)).reshape(seq_count, blocks_dev * block_size)
    return (count_left, beta_out, log_scales)


def solution(mesh):
    in_specs = (
        P(None, "groups"),
        P("groups", "blk"),
        P("groups", "blk"),
        P(),
        P("blk", None, None),
        P("blk", None, None),
    )
    out_specs = (P(("groups", "blk"), None, None), P("groups", "blk"), P(None, "groups"))
    devices = mesh.shape["blk"]

    def body(*operands):
        if fused_fits(operands[1].shape[0], *operands[4].shape[:2]):
            return on_device_fused(devices, *operands)
        return on_device(*operands)

    return jax.shard_map(
        body, mesh=mesh, in_specs=in_specs, out_specs=out_specs, check_vma=False
    )
```

```python
import functools

import jax
import jax.numpy as jnp
from jax import lax
from jax.experimental import pallas as pl
from jax.experimental.pallas import tpu as pltpu
from jax.sharding import PartitionSpec as P

LANES = 128
SUBLANES = 8
MIB = 1 << 20


def dot(x, w, w_dim):
    return lax.dot_general(
        x, w, (((1,), (w_dim,)), ((), ())), preferred_element_type=jnp.float32
    )


def messages_kernel(
    devices,
    window,
    alpha_hbm,
    beta_hbm,
    left_hbm,
    right_hbm,
    rows_ref,
    paths_hbm,
    values_hbm,
    beta_out_hbm,
    totals_ref,
    post_ref,
    mean_ref,
    left,
    right,
    alpha_first,
    alphas,
    beta_flat,
    prior_last_step,
    values,
    paths,
    staged,
    unpacked,
    outbox,
    inbox,
    small_out,
    small_in,
    post_sums,
    left_sem,
    right_sem,
    message_sem,
    out_sem,
    own_sem,
    send_sem,
    recv_sem,
    small_send_sem,
    small_recv_sem,
):
    blocks, size, _ = left.shape
    seqs = alpha_first.shape[0]
    states = size * size
    tiles = size // LANES
    group = LANES // blocks
    steps = window - 1
    chunks = left_sem.shape[0]
    per_chunk = blocks // chunks
    me = lax.axis_index("blk")

    def loop(count, body, start=0, unroll=1):
        def wrapped(i, carry):
            body(i)
            return carry

        lax.fori_loop(start, count, wrapped, 0, unroll=unroll)

    def chunk_copy(hbm, ref, sem, c):
        part = pl.ds(c * per_chunk, per_chunk)
        return pltpu.make_async_copy(hbm.at[part], ref.at[part], sem.at[c])

    alpha_copy = pltpu.make_async_copy(alpha_hbm, alpha_first, message_sem.at[0])
    beta_copy = pltpu.make_async_copy(beta_hbm, beta_flat, message_sem.at[1])
    alpha_copy.start()
    loop(chunks, lambda c: chunk_copy(right_hbm, right, right_sem, c).start())
    beta_copy.start()
    loop(chunks, lambda c: chunk_copy(left_hbm, left, left_sem, c).start())

    barrier = pltpu.get_barrier_semaphore()

    def greet(off):
        pl.semaphore_signal(
            barrier,
            inc=1,
            device_id={"blk": lax.rem(me + off, devices)},
            device_id_type=pl.DeviceIdType.MESH,
        )

    loop(devices, greet, 1)
    pl.semaphore_wait(barrier, devices - 1)

    def block_copy(chain, par, off, landing):
        other = lax.rem(me + off, devices)
        return pltpu.make_async_remote_copy(
            src_ref=outbox.at[chain, pl.ds(pl.multiple_of(other * blocks, blocks), blocks)],
            dst_ref=inbox.at[chain, par, landing(other)],
            send_sem=send_sem.at[chain, off],
            recv_sem=recv_sem.at[chain, par, landing(other)],
            device_id={"blk": other},
            device_id_type=pl.DeviceIdType.MESH,
        )

    def own_copy(chain, par):
        return pltpu.make_async_copy(
            outbox.at[chain, pl.ds(pl.multiple_of(me * blocks, blocks), blocks)],
            inbox.at[chain, par, me],
            own_sem.at[chain],
        )

    def sent(chain, par):
        loop(devices, lambda off: block_copy(chain, par, off, lambda other: me).wait_send(), 1)

    def pack_and_send(chain, par):
        def pack(j):
            lanes = pl.ds(pl.multiple_of(j * LANES, LANES), LANES)
            for k in range(tiles):
                picked = [
                    staged[k, pl.ds(j * group + c, blocks, stride=seqs), :] for c in range(group)
                ]
                turned = jnp.transpose(jnp.concatenate(picked, axis=0))
                outbox[chain, k * LANES : (k + 1) * LANES, lanes] = turned.astype(jnp.bfloat16)

        loop(seqs // group, pack)
        loop(devices, lambda i: block_copy(chain, par, lax.rem(i * 7, devices), lambda other: me).start(), 1)
        own_copy(chain, par).start()

    def receive(chain, par):
        own_copy(chain, par).wait()
        loop(devices, lambda off: block_copy(chain, par, off, lambda other: other).wait_recv(), 1)
        place = lax.broadcasted_iota(jnp.int32, (blocks, LANES), 1) // blocks

        def merge(pieces):
            merged = pieces[0]
            for g in range(1, group):
                merged = jnp.where(place == g, pieces[g], merged)
            return merged

        def unpack(j):
            lanes = pl.ds(pl.multiple_of(j * LANES, LANES), LANES)
            for k in range(tiles):
                came = [
                    inbox[chain, par, k * group + i, :, lanes].astype(jnp.float32)
                    for i in range(group)
                ]
                shifted = []
                for s in range(group):
                    mixed = merge([came[(g + s) % group] for g in range(group)])
                    shifted.append(pltpu.roll(mixed, s * blocks, 1) if s else mixed)
                for c in range(group):
                    unpacked[k, pl.ds(j * group + c, blocks, stride=seqs), :] = merge(
                        [shifted[(i - c) % group] for i in range(group)]
                    )

        loop(seqs // group, unpack)

    def small_copy(kind, slot, off, landing):
        other = lax.rem(me + off, devices)
        return pltpu.make_async_remote_copy(
            src_ref=small_out.at[kind],
            dst_ref=small_in.at[slot, landing(other)],
            send_sem=small_send_sem.at[kind, off],
            recv_sem=small_recv_sem.at[slot, landing(other)],
            device_id={"blk": other},
            device_id_type=pl.DeviceIdType.MESH,
        )

    def small_sent(kind, slot):
        loop(devices, lambda off: small_copy(kind, slot, off, lambda other: me).wait_send(), 1)

    def small_send(kind, slot, columns):
        lane = lax.broadcasted_iota(jnp.int32, (SUBLANES, LANES), 1)
        tile = jnp.zeros((SUBLANES, LANES), jnp.float32)
        for c, column in enumerate(columns):
            for i in range(seqs // SUBLANES):
                part = column[i * SUBLANES : (i + 1) * SUBLANES, :]
                tile = jnp.where(lane == c * (seqs // SUBLANES) + i, part, tile)
        small_out[kind] = tile
        small_in[slot, me] = tile
        loop(devices, lambda off: small_copy(kind, slot, off, lambda other: me).start(), 1)

    def small_receive(kind, slot, count):
        loop(devices, lambda off: small_copy(kind, slot, off, lambda other: other).wait_recv(), 1)
        total = jnp.sum(small_in[slot], axis=0)
        per = seqs // SUBLANES
        return [
            jnp.concatenate(
                [total[:, c * per + i : c * per + i + 1] for i in range(per)], axis=0
            )
            for c in range(count)
        ]

    def flat(b):
        return pl.ds(pl.multiple_of(b * size, size), size)

    def block_rows(b):
        return pl.ds(pl.multiple_of(b * seqs, seqs), seqs)

    def stage(b, result):
        for k in range(tiles):
            staged[k, block_rows(b), :] = result[:, k * LANES : (k + 1) * LANES]

    def arrived(b):
        return jnp.concatenate(
            [unpacked[k, block_rows(b), :] for k in range(tiles)], axis=1
        ).astype(jnp.bfloat16)

    def narrow(wide):
        total = wide[:, :LANES]
        for k in range(1, tiles):
            total = total + wide[:, k * LANES : (k + 1) * LANES]
        return total

    zero = jnp.zeros((seqs, LANES), jnp.float32)

    def column(total):
        return jnp.sum(total, axis=1, keepdims=True)

    alpha_copy.wait()

    def first_path(c):
        chunk_copy(right_hbm, right, right_sem, c).wait()
        loop(
            per_chunk,
            lambda i: stage(
                c * per_chunk + i,
                dot(alpha_first[:, flat(c * per_chunk + i)], right[c * per_chunk + i], 0),
            ),
        )

    loop(chunks, first_path)
    pack_and_send(0, 0)
    even = jnp.full((seqs, 1), states / devices, jnp.float32)
    small_send(0, 0, [even])

    beta_copy.wait()

    def first_back(c):
        chunk_copy(left_hbm, left, left_sem, c).wait()

        def one(i):
            b = c * per_chunk + i
            emitted = rows_ref[steps].astype(jnp.float32) * beta_flat[:, flat(b)].astype(
                jnp.float32
            )
            values[steps, b] = emitted.astype(jnp.bfloat16)
            stage(b, dot(values[steps, b], left[b], 1))

        loop(per_chunk, one)

    loop(chunks, first_back)
    pack_and_send(1, 0)
    small_send(1, 2, [even])

    def values_copy(t):
        return pltpu.make_async_copy(values.at[t], values_hbm.at[:, t], out_sem.at[0, t])

    def paths_copy(t):
        return pltpu.make_async_copy(paths.at[t], paths_hbm.at[:, t], out_sem.at[1, t])

    values_copy(steps).start()

    def keep_mean(ref, index, total):
        mean = total * (1.0 / states)
        ref[index] = jnp.broadcast_to(mean, (seqs, LANES))
        return 1.0 / mean

    def step_body(k):
        par, later = lax.rem(k, 2), lax.rem(k + 1, 2)

        receive(0, par)
        (total,) = small_receive(0, par, 1)
        scale = keep_mean(totals_ref, k, total)

        def forward(b, acc):
            path = arrived(b)
            paths[k, b] = path
            ahead = dot(path, left[b], 0)
            weighted = ahead * (rows_ref[k].astype(jnp.float32) * scale)
            alphas[k, b] = weighted.astype(jnp.bfloat16)
            return acc + narrow(weighted)

        acc = lax.fori_loop(0, blocks, forward, zero, unroll=2)
        small_sent(0, par)
        small_send(0, later, [column(acc)])
        paths_copy(k).start()
        loop(blocks, lambda b: stage(b, dot(alphas[k, b], right[b], 0)), unroll=2)
        sent(0, par)
        pack_and_send(0, later)

        receive(1, par)
        (total,) = small_receive(1, 2 + par, 1)
        scale = keep_mean(mean_ref, steps - k, total)

        def backward(b, accs):
            prior = dot(arrived(b), right[b], 1) * scale
            prior_last_step[lax.min(k, 1), b] = prior.astype(jnp.bfloat16)
            emitted = rows_ref[steps - 1 - k].astype(jnp.float32) * prior
            values[steps - 1 - k, b] = emitted.astype(jnp.bfloat16)
            both = alphas[post_source(k), b].astype(jnp.float32) * prior
            return accs[0] + narrow(prior), accs[1] + narrow(both)

        acc, post = lax.fori_loop(0, blocks, backward, (zero, zero), unroll=2)
        small_sent(1, 2 + par)
        small_send(1, 2 + later, [column(acc)])
        post_sums[steps - k] = post
        values_copy(steps - 1 - k).start()
        loop(
            blocks,
            lambda b: stage(b, dot(values[steps - 1 - k, b], left[b], 1)),
            unroll=2,
        )
        sent(1, par)
        pack_and_send(1, later)

    def post_source(k):
        return lax.min(steps - 1 - k, k)

    loop(steps, step_body)
    par = steps % 2

    for late in range(steps):
        if steps - 1 - late > late:

            def late_post(b, acc):
                both = alphas[steps - 1 - late, b].astype(jnp.float32) * prior_last_step[
                    late, b
                ].astype(jnp.float32)
                return acc + narrow(both)

            post_sums[steps - late] = lax.fori_loop(0, blocks, late_post, zero)

    receive(0, par)
    (total,) = small_receive(0, par, 1)
    keep_mean(totals_ref, steps, total)

    def last_path(b):
        paths[steps, b] = arrived(b)

    loop(blocks, last_path)
    paths_copy(steps).start()

    receive(1, par)
    (total,) = small_receive(1, 2 + par, 1)
    scale = keep_mean(mean_ref, 0, total)

    def last_prior(b, accs):
        prior = dot(arrived(b), right[b], 1) * scale
        stage(b, prior)
        both = alpha_first[:, flat(b)].astype(jnp.float32) * prior
        return accs[0] + narrow(prior), accs[1] + narrow(both)

    acc, post = lax.fori_loop(0, blocks, last_prior, (zero, zero), unroll=2)
    post_sums[0] = post
    small_send(2, 4, [column(acc)] + [column(post_sums[t]) for t in range(window)])
    found = small_receive(2, 4, 1 + window)
    norm = states / found[0]
    for t in range(window):
        post_ref[t] = jnp.broadcast_to(found[1 + t], (seqs, LANES))

    def last_beta(b):
        wide = jnp.concatenate([staged[k, block_rows(b), :] for k in range(tiles)], axis=1)
        beta_flat[:, flat(b)] = (wide * norm).astype(jnp.bfloat16)

    loop(blocks, last_beta)
    result = pltpu.make_async_copy(beta_flat, beta_out_hbm, message_sem.at[0])
    result.start()
    for t in range(window):
        values_copy(t).wait()
        paths_copy(t).wait()
    sent(0, par)
    sent(1, par)
    small_sent(0, par)
    small_sent(1, 2 + par)
    small_sent(2, 4)
    result.wait()


def counts_kernel(factor, post_ref, mean_ref, left_ref, paths_ref, values_ref, count_ref):
    over_post, over_mean = 1.0 / post_ref[:, :1], 1.0 / mean_ref[:, :1]
    for i in range(left_ref.shape[0]):
        scaled = paths_ref[i].astype(jnp.float32) * over_post * over_mean
        tally = lax.dot_general(
            scaled.astype(jnp.bfloat16),
            values_ref[i],
            (((0,), (0,)), ((), ())),
            preferred_element_type=jnp.float32,
        )
        count_ref[i] = (left_ref[i].astype(jnp.float32) * tally * factor).astype(jnp.bfloat16)


def on_device_fused(devices, tokens, alpha_start, beta_in, emission, left_factor, right_factor):
    blocks, size, _ = left_factor.shape
    seqs = alpha_start.shape[0]
    window = tokens.shape[0]
    vocab = emission.shape[0]
    steps = window - 1
    picked = tokens.reshape(-1)[:, None] == lax.broadcasted_iota(
        jnp.int32, (window * seqs, vocab), 1
    )
    rows = jnp.dot(
        picked.astype(jnp.bfloat16), emission, preferred_element_type=jnp.float32
    ).reshape(window, seqs, size)
    any_space = pl.BlockSpec(memory_space=pl.ANY)
    in_vmem = pl.BlockSpec(memory_space=pltpu.VMEM)
    bf16, f32 = jnp.bfloat16, jnp.float32
    tiles = size // LANES
    chunks = 4
    per_step = jax.ShapeDtypeStruct((window, seqs, LANES), f32)
    kept = jax.ShapeDtypeStruct((blocks, window, seqs, size), bf16)
    messages = (blocks, seqs, size)
    turned = (tiles, blocks * seqs, LANES)
    paths, values, beta_out, totals, post, mean = pl.pallas_call(
        functools.partial(messages_kernel, devices, window),
        out_shape=(
            kept,
            kept,
            jax.ShapeDtypeStruct(beta_in.shape, bf16),
            per_step,
            per_step,
            per_step,
        ),
        in_specs=[any_space] * 4 + [in_vmem],
        out_specs=(any_space,) * 3 + (in_vmem,) * 3,
        scratch_shapes=[
            pltpu.VMEM(left_factor.shape, bf16),
            pltpu.VMEM(right_factor.shape, bf16),
            pltpu.VMEM(alpha_start.shape, bf16),
            pltpu.VMEM((steps,) + messages, bf16),
            pltpu.VMEM(beta_in.shape, bf16),
            pltpu.VMEM((2,) + messages, bf16),
            pltpu.VMEM((window,) + messages, bf16),
            pltpu.VMEM((window,) + messages, bf16),
            pltpu.VMEM(turned, f32),
            pltpu.VMEM(turned, f32),
            pltpu.VMEM((2, size, seqs * blocks), bf16),
            pltpu.VMEM((2, 2, devices, blocks, seqs * blocks), bf16),
            pltpu.VMEM((3, SUBLANES, LANES), f32),
            pltpu.VMEM((5, devices, SUBLANES, LANES), f32),
            pltpu.VMEM((window, seqs, LANES), f32),
            pltpu.SemaphoreType.DMA((chunks,)),
            pltpu.SemaphoreType.DMA((chunks,)),
            pltpu.SemaphoreType.DMA((2,)),
            pltpu.SemaphoreType.DMA((2, window)),
            pltpu.SemaphoreType.DMA((2,)),
            pltpu.SemaphoreType.DMA((2, devices)),
            pltpu.SemaphoreType.DMA((2, 2, devices)),
            pltpu.SemaphoreType.DMA((3, devices)),
            pltpu.SemaphoreType.DMA((5, devices)),
        ],
        compiler_params=pltpu.CompilerParams(
            collective_id=0, has_side_effects=True, vmem_limit_bytes=62 * MIB
        ),
    )(alpha_start, beta_in, left_factor, right_factor, rows)
    per_call = 4
    rows_all = window * seqs
    factor = size * (size * size / seqs)
    scale_spec = pl.BlockSpec((rows_all, LANES), lambda b: (0, 0))
    factor_spec = pl.BlockSpec((per_call, size, size), lambda b: (b, 0, 0))
    kept_spec = pl.BlockSpec((per_call, rows_all, size), lambda b: (b, 0, 0))
    count_left = pl.pallas_call(
        functools.partial(counts_kernel, factor),
        grid=(blocks // per_call,),
        out_shape=jax.ShapeDtypeStruct(left_factor.shape, bf16),
        in_specs=[scale_spec, scale_spec, factor_spec, kept_spec, kept_spec],
        out_specs=factor_spec,
        compiler_params=pltpu.CompilerParams(vmem_limit_bytes=60 * MIB),
    )(
        post.reshape(rows_all, LANES),
        mean.reshape(rows_all, LANES),
        left_factor,
        paths.reshape(blocks, rows_all, size),
        values.reshape(blocks, rows_all, size),
    )
    log_scales = jnp.log(totals[1:, :, 0])
    return count_left, beta_out, log_scales


def fused_fits(seqs, blocks, size):
    if blocks % 16 or LANES % blocks or size % LANES or seqs % 16:
        return False
    return seqs % (LANES // blocks) == 0


def on_device(tokens, alpha_start, beta_in, emission, left_factor, right_factor):
    blocks_dev, block_size, _ = left_factor.shape
    seq_count = alpha_start.shape[0]
    window = tokens.shape[0]
    vocab_size = emission.shape[0]
    states = block_size * block_size

    def emission_rows(step):
        picked = tokens[step][:, None] == lax.broadcasted_iota(
            jnp.int32, (seq_count, vocab_size), 1
        )
        rows = jnp.dot(picked.astype(jnp.bfloat16), emission, preferred_element_type=jnp.float32)
        return rows[None, :, :]

    def path_sums(message):
        return jnp.einsum(
            "rns,rsp->rnp", message, right_factor, preferred_element_type=jnp.float32
        ).astype(jnp.bfloat16)

    forward_msg = jnp.transpose(alpha_start.reshape(seq_count, blocks_dev, block_size), (1, 0, 2))
    forwards = [forward_msg]
    received = []
    log_rows = []
    for step in range(1, window):
        arrived = lax.all_to_all(
            path_sums(forward_msg), "blk", split_axis=2, concat_axis=0, tiled=True
        )
        turned_paths = jnp.transpose(arrived, (2, 1, 0))
        received.append(turned_paths)
        ahead = jnp.einsum(
            "pnr,prq->pnq", turned_paths, left_factor, preferred_element_type=jnp.float32
        )
        weighted = ahead * emission_rows(step - 1)
        forward_total = lax.psum(jnp.sum(weighted, axis=(0, 2)), "blk")
        log_rows.append(jnp.log(forward_total / states))
        forward_msg = (states * weighted / forward_total[None, :, None]).astype(jnp.bfloat16)
        forwards.append(forward_msg)
    last_send = path_sums(forward_msg)
    received.append(
        jnp.transpose(
            lax.all_to_all(last_send, "blk", split_axis=2, concat_axis=0, tiled=True), (2, 1, 0)
        )
    )
    backward_msg = jnp.transpose(beta_in.reshape(seq_count, blocks_dev, block_size), (1, 0, 2))
    weights = []
    values = []
    for step in range(window, 0, -1):
        emitted = (emission_rows(step - 1) * backward_msg).astype(jnp.bfloat16)
        back_sums = jnp.einsum(
            "pnq,prq->pnr", emitted, left_factor, preferred_element_type=jnp.float32
        ).astype(jnp.bfloat16)
        if step == window:
            turned = lax.all_to_all(back_sums, "blk", split_axis=2, concat_axis=0, tiled=True)
        else:
            turned = lax.all_to_all(back_sums, "blk", split_axis=2, concat_axis=0, tiled=True)
        turned_back = jnp.transpose(turned, (2, 1, 0))
        prior = jnp.einsum(
            "rnp,rsp->rns", turned_back, right_factor, preferred_element_type=jnp.float32
        )
        norm_total, posterior_total = lax.psum(
            (jnp.sum(prior, axis=(0, 2)), jnp.sum(forwards[step - 1] * prior, axis=(0, 2))), "blk"
        )
        weights.append(
            (received[step - 1].astype(jnp.float32) / posterior_total[None, :, None]).astype(
                jnp.bfloat16
            )
        )
        values.append(emitted)
        backward_msg = (states * prior / norm_total[None, :, None]).astype(jnp.bfloat16)
    stacked_weights = jnp.concatenate(weights, axis=1)
    stacked_values = jnp.concatenate(values, axis=1)
    tally = jnp.einsum(
        "pnr,pnq->prq", stacked_weights, stacked_values, preferred_element_type=jnp.float32
    )
    count_left = (left_factor * tally * (block_size * states / seq_count)).astype(jnp.bfloat16)
    log_scales = jnp.stack(log_rows, axis=0)
    beta_out = jnp.transpose(backward_msg, (1, 0, 2)).reshape(seq_count, blocks_dev * block_size)
    return (count_left, beta_out, log_scales)


def solution(mesh):
    in_specs = (
        P(None, "groups"),
        P("groups", "blk"),
        P("groups", "blk"),
        P(),
        P("blk", None, None),
        P("blk", None, None),
    )
    out_specs = (P(("groups", "blk"), None, None), P("groups", "blk"), P(None, "groups"))
    devices = mesh.shape["blk"]

    def body(*operands):
        if fused_fits(operands[1].shape[0], *operands[4].shape[:2]):
            return on_device_fused(devices, *operands)
        return on_device(*operands)

    return jax.shard_map(
        body, mesh=mesh, in_specs=in_specs, out_specs=out_specs, check_vma=False
    )
```

```python
import functools

import jax
import jax.numpy as jnp
from jax import lax
from jax.experimental import pallas as pl
from jax.experimental.pallas import tpu as pltpu
from jax.sharding import PartitionSpec as P

LANES = 128
SUBLANES = 8
MIB = 1 << 20


def dot(x, w, w_dim):
    return lax.dot_general(
        x, w, (((1,), (w_dim,)), ((), ())), preferred_element_type=jnp.float32
    )


def messages_kernel(
    devices,
    window,
    alpha_hbm,
    beta_hbm,
    left_hbm,
    right_hbm,
    rows_ref,
    paths_hbm,
    values_hbm,
    beta_out_hbm,
    totals_ref,
    post_ref,
    mean_ref,
    left,
    right,
    alpha_first,
    alphas,
    beta_flat,
    prior_last_step,
    values,
    paths,
    staged,
    unpacked,
    outbox,
    inbox,
    small_out,
    small_in,
    post_sums,
    left_sem,
    right_sem,
    message_sem,
    out_sem,
    own_sem,
    send_sem,
    recv_sem,
    small_send_sem,
    small_recv_sem,
):
    blocks, size, _ = left.shape
    seqs = alpha_first.shape[0]
    states = size * size
    tiles = size // LANES
    group = LANES // blocks
    steps = window - 1
    chunks = left_sem.shape[0]
    per_chunk = blocks // chunks
    me = lax.axis_index("blk")

    def loop(count, body, start=0, unroll=1):
        def wrapped(i, carry):
            body(i)
            return carry

        lax.fori_loop(start, count, wrapped, 0, unroll=unroll)

    def chunk_copy(hbm, ref, sem, c):
        part = pl.ds(c * per_chunk, per_chunk)
        return pltpu.make_async_copy(hbm.at[part], ref.at[part], sem.at[c])

    alpha_copy = pltpu.make_async_copy(alpha_hbm, alpha_first, message_sem.at[0])
    beta_copy = pltpu.make_async_copy(beta_hbm, beta_flat, message_sem.at[1])
    alpha_copy.start()
    loop(chunks, lambda c: chunk_copy(right_hbm, right, right_sem, c).start())
    beta_copy.start()
    loop(chunks, lambda c: chunk_copy(left_hbm, left, left_sem, c).start())

    barrier = pltpu.get_barrier_semaphore()

    def greet(off):
        pl.semaphore_signal(
            barrier,
            inc=1,
            device_id={"blk": lax.rem(me + off, devices)},
            device_id_type=pl.DeviceIdType.MESH,
        )

    loop(devices, greet, 1)
    pl.semaphore_wait(barrier, devices - 1)

    def block_copy(chain, par, off, landing):
        other = lax.rem(me + off, devices)
        return pltpu.make_async_remote_copy(
            src_ref=outbox.at[chain, pl.ds(pl.multiple_of(other * blocks, blocks), blocks)],
            dst_ref=inbox.at[chain, par, landing(other)],
            send_sem=send_sem.at[chain, off],
            recv_sem=recv_sem.at[chain, par, landing(other)],
            device_id={"blk": other},
            device_id_type=pl.DeviceIdType.MESH,
        )

    def own_copy(chain, par):
        return pltpu.make_async_copy(
            outbox.at[chain, pl.ds(pl.multiple_of(me * blocks, blocks), blocks)],
            inbox.at[chain, par, me],
            own_sem.at[chain],
        )

    def sent(chain, par):
        loop(devices, lambda off: block_copy(chain, par, off, lambda other: me).wait_send(), 1)

    def pack_and_send(chain, par):
        def pack(j):
            lanes = pl.ds(pl.multiple_of(j * LANES, LANES), LANES)
            for k in range(tiles):
                picked = [
                    staged[k, pl.ds(j * group + c, blocks, stride=seqs), :] for c in range(group)
                ]
                turned = jnp.transpose(jnp.concatenate(picked, axis=0))
                outbox[chain, k * LANES : (k + 1) * LANES, lanes] = turned.astype(jnp.bfloat16)

        loop(seqs // group, pack, unroll=2)
        loop(devices, lambda i: block_copy(chain, par, lax.rem(i * 7, devices), lambda other: me).start(), 1)
        own_copy(chain, par).start()

    def receive(chain, par):
        own_copy(chain, par).wait()
        loop(devices, lambda off: block_copy(chain, par, off, lambda other: other).wait_recv(), 1)
        place = lax.broadcasted_iota(jnp.int32, (blocks, LANES), 1) // blocks

        def merge(pieces):
            merged = pieces[0]
            for g in range(1, group):
                merged = jnp.where(place == g, pieces[g], merged)
            return merged

        def unpack(j):
            lanes = pl.ds(pl.multiple_of(j * LANES, LANES), LANES)
            for k in range(tiles):
                came = [
                    inbox[chain, par, k * group + i, :, lanes].astype(jnp.float32)
                    for i in range(group)
                ]
                shifted = []
                for s in range(group):
                    mixed = merge([came[(g + s) % group] for g in range(group)])
                    shifted.append(pltpu.roll(mixed, s * blocks, 1) if s else mixed)
                for c in range(group):
                    unpacked[k, pl.ds(j * group + c, blocks, stride=seqs), :] = merge(
                        [shifted[(i - c) % group] for i in range(group)]
                    )

        loop(seqs // group, unpack, unroll=2)

    def small_copy(kind, slot, off, landing):
        other = lax.rem(me + off, devices)
        return pltpu.make_async_remote_copy(
            src_ref=small_out.at[kind],
            dst_ref=small_in.at[slot, landing(other)],
            send_sem=small_send_sem.at[kind, off],
            recv_sem=small_recv_sem.at[slot, landing(other)],
            device_id={"blk": other},
            device_id_type=pl.DeviceIdType.MESH,
        )

    def small_sent(kind, slot):
        loop(devices, lambda off: small_copy(kind, slot, off, lambda other: me).wait_send(), 1)

    def small_send(kind, slot, columns):
        lane = lax.broadcasted_iota(jnp.int32, (SUBLANES, LANES), 1)
        tile = jnp.zeros((SUBLANES, LANES), jnp.float32)
        for c, column in enumerate(columns):
            for i in range(seqs // SUBLANES):
                part = column[i * SUBLANES : (i + 1) * SUBLANES, :]
                tile = jnp.where(lane == c * (seqs // SUBLANES) + i, part, tile)
        small_out[kind] = tile
        small_in[slot, me] = tile
        loop(devices, lambda off: small_copy(kind, slot, off, lambda other: me).start(), 1)

    def small_receive(kind, slot, count):
        loop(devices, lambda off: small_copy(kind, slot, off, lambda other: other).wait_recv(), 1)
        total = jnp.sum(small_in[slot], axis=0)
        per = seqs // SUBLANES
        return [
            jnp.concatenate(
                [total[:, c * per + i : c * per + i + 1] for i in range(per)], axis=0
            )
            for c in range(count)
        ]

    def flat(b):
        return pl.ds(pl.multiple_of(b * size, size), size)

    def block_rows(b):
        return pl.ds(pl.multiple_of(b * seqs, seqs), seqs)

    def stage(b, result):
        for k in range(tiles):
            staged[k, block_rows(b), :] = result[:, k * LANES : (k + 1) * LANES]

    def arrived(b):
        return jnp.concatenate(
            [unpacked[k, block_rows(b), :] for k in range(tiles)], axis=1
        ).astype(jnp.bfloat16)

    def narrow(wide):
        total = wide[:, :LANES]
        for k in range(1, tiles):
            total = total + wide[:, k * LANES : (k + 1) * LANES]
        return total

    zero = jnp.zeros((seqs, LANES), jnp.float32)

    def column(total):
        return jnp.sum(total, axis=1, keepdims=True)

    alpha_copy.wait()

    def first_path(c):
        chunk_copy(right_hbm, right, right_sem, c).wait()
        loop(
            per_chunk,
            lambda i: stage(
                c * per_chunk + i,
                dot(alpha_first[:, flat(c * per_chunk + i)], right[c * per_chunk + i], 0),
            ),
            unroll=2,
        )

    loop(chunks, first_path)
    pack_and_send(0, 0)
    even = jnp.full((seqs, 1), states / devices, jnp.float32)
    small_send(0, 0, [even])

    beta_copy.wait()

    def first_back(c):
        chunk_copy(left_hbm, left, left_sem, c).wait()

        def one(i):
            b = c * per_chunk + i
            emitted = rows_ref[steps].astype(jnp.float32) * beta_flat[:, flat(b)].astype(
                jnp.float32
            )
            values[steps, b] = emitted.astype(jnp.bfloat16)
            stage(b, dot(values[steps, b], left[b], 1))

        loop(per_chunk, one, unroll=2)

    loop(chunks, first_back)
    pack_and_send(1, 0)
    small_send(1, 2, [even])

    def values_copy(t):
        return pltpu.make_async_copy(values.at[t], values_hbm.at[:, t], out_sem.at[0, t])

    def paths_copy(t):
        return pltpu.make_async_copy(paths.at[t], paths_hbm.at[:, t], out_sem.at[1, t])

    values_copy(steps).start()

    def keep_mean(ref, index, total):
        mean = total * (1.0 / states)
        ref[index] = jnp.broadcast_to(mean, (seqs, LANES))
        return 1.0 / mean

    def step_body(k):
        par, later = lax.rem(k, 2), lax.rem(k + 1, 2)

        receive(0, par)
        (total,) = small_receive(0, par, 1)
        scale = keep_mean(totals_ref, k, total)

        def forward(b, acc):
            path = arrived(b)
            paths[k, b] = path
            ahead = dot(path, left[b], 0)
            weighted = ahead * (rows_ref[k].astype(jnp.float32) * scale)
            alphas[k, b] = weighted.astype(jnp.bfloat16)
            return acc + narrow(weighted)

        acc = lax.fori_loop(0, blocks, forward, zero, unroll=2)
        small_sent(0, par)
        small_send(0, later, [column(acc)])
        paths_copy(k).start()
        loop(blocks, lambda b: stage(b, dot(alphas[k, b], right[b], 0)), unroll=2)
        sent(0, par)
        pack_and_send(0, later)

        receive(1, par)
        (total,) = small_receive(1, 2 + par, 1)
        scale = keep_mean(mean_ref, steps - k, total)

        def backward(b, accs):
            prior = dot(arrived(b), right[b], 1) * scale
            prior_last_step[lax.min(k, 1), b] = prior.astype(jnp.bfloat16)
            emitted = rows_ref[steps - 1 - k].astype(jnp.float32) * prior
            values[steps - 1 - k, b] = emitted.astype(jnp.bfloat16)
            both = alphas[post_source(k), b].astype(jnp.float32) * prior
            return accs[0] + narrow(prior), accs[1] + narrow(both)

        acc, post = lax.fori_loop(0, blocks, backward, (zero, zero), unroll=2)
        small_sent(1, 2 + par)
        small_send(1, 2 + later, [column(acc)])
        post_sums[steps - k] = post
        values_copy(steps - 1 - k).start()
        loop(
            blocks,
            lambda b: stage(b, dot(values[steps - 1 - k, b], left[b], 1)),
            unroll=2,
        )
        sent(1, par)
        pack_and_send(1, later)

    def post_source(k):
        return lax.min(steps - 1 - k, k)

    loop(steps, step_body)
    par = steps % 2

    for late in range(steps):
        if steps - 1 - late > late:

            def late_post(b, acc):
                both = alphas[steps - 1 - late, b].astype(jnp.float32) * prior_last_step[
                    late, b
                ].astype(jnp.float32)
                return acc + narrow(both)

            post_sums[steps - late] = lax.fori_loop(0, blocks, late_post, zero)

    receive(0, par)
    (total,) = small_receive(0, par, 1)
    keep_mean(totals_ref, steps, total)

    def last_path(b):
        paths[steps, b] = arrived(b)

    loop(blocks, last_path)
    paths_copy(steps).start()

    receive(1, par)
    (total,) = small_receive(1, 2 + par, 1)
    scale = keep_mean(mean_ref, 0, total)

    def last_prior(b, accs):
        prior = dot(arrived(b), right[b], 1) * scale
        stage(b, prior)
        both = alpha_first[:, flat(b)].astype(jnp.float32) * prior
        return accs[0] + narrow(prior), accs[1] + narrow(both)

    acc, post = lax.fori_loop(0, blocks, last_prior, (zero, zero), unroll=2)
    post_sums[0] = post
    small_send(2, 4, [column(acc)] + [column(post_sums[t]) for t in range(window)])
    found = small_receive(2, 4, 1 + window)
    norm = states / found[0]
    for t in range(window):
        post_ref[t] = jnp.broadcast_to(found[1 + t], (seqs, LANES))

    def last_beta(b):
        wide = jnp.concatenate([staged[k, block_rows(b), :] for k in range(tiles)], axis=1)
        beta_flat[:, flat(b)] = (wide * norm).astype(jnp.bfloat16)

    loop(blocks, last_beta)
    result = pltpu.make_async_copy(beta_flat, beta_out_hbm, message_sem.at[0])
    result.start()
    for t in range(window):
        values_copy(t).wait()
        paths_copy(t).wait()
    sent(0, par)
    sent(1, par)
    small_sent(0, par)
    small_sent(1, 2 + par)
    small_sent(2, 4)
    result.wait()


def counts_kernel(factor, post_ref, mean_ref, left_ref, paths_ref, values_ref, count_ref):
    over_post, over_mean = 1.0 / post_ref[:, :1], 1.0 / mean_ref[:, :1]
    for i in range(left_ref.shape[0]):
        scaled = paths_ref[i].astype(jnp.float32) * over_post * over_mean
        tally = lax.dot_general(
            scaled.astype(jnp.bfloat16),
            values_ref[i],
            (((0,), (0,)), ((), ())),
            preferred_element_type=jnp.float32,
        )
        count_ref[i] = (left_ref[i].astype(jnp.float32) * tally * factor).astype(jnp.bfloat16)


def on_device_fused(devices, tokens, alpha_start, beta_in, emission, left_factor, right_factor):
    blocks, size, _ = left_factor.shape
    seqs = alpha_start.shape[0]
    window = tokens.shape[0]
    vocab = emission.shape[0]
    steps = window - 1
    picked = tokens.reshape(-1)[:, None] == lax.broadcasted_iota(
        jnp.int32, (window * seqs, vocab), 1
    )
    rows = jnp.dot(
        picked.astype(jnp.bfloat16), emission, preferred_element_type=jnp.float32
    ).reshape(window, seqs, size)
    any_space = pl.BlockSpec(memory_space=pl.ANY)
    in_vmem = pl.BlockSpec(memory_space=pltpu.VMEM)
    bf16, f32 = jnp.bfloat16, jnp.float32
    tiles = size // LANES
    chunks = 4
    per_step = jax.ShapeDtypeStruct((window, seqs, LANES), f32)
    kept = jax.ShapeDtypeStruct((blocks, window, seqs, size), bf16)
    messages = (blocks, seqs, size)
    turned = (tiles, blocks * seqs, LANES)
    paths, values, beta_out, totals, post, mean = pl.pallas_call(
        functools.partial(messages_kernel, devices, window),
        out_shape=(
            kept,
            kept,
            jax.ShapeDtypeStruct(beta_in.shape, bf16),
            per_step,
            per_step,
            per_step,
        ),
        in_specs=[any_space] * 4 + [in_vmem],
        out_specs=(any_space,) * 3 + (in_vmem,) * 3,
        scratch_shapes=[
            pltpu.VMEM(left_factor.shape, bf16),
            pltpu.VMEM(right_factor.shape, bf16),
            pltpu.VMEM(alpha_start.shape, bf16),
            pltpu.VMEM((steps,) + messages, bf16),
            pltpu.VMEM(beta_in.shape, bf16),
            pltpu.VMEM((2,) + messages, bf16),
            pltpu.VMEM((window,) + messages, bf16),
            pltpu.VMEM((window,) + messages, bf16),
            pltpu.VMEM(turned, f32),
            pltpu.VMEM(turned, f32),
            pltpu.VMEM((2, size, seqs * blocks), bf16),
            pltpu.VMEM((2, 2, devices, blocks, seqs * blocks), bf16),
            pltpu.VMEM((3, SUBLANES, LANES), f32),
            pltpu.VMEM((5, devices, SUBLANES, LANES), f32),
            pltpu.VMEM((window, seqs, LANES), f32),
            pltpu.SemaphoreType.DMA((chunks,)),
            pltpu.SemaphoreType.DMA((chunks,)),
            pltpu.SemaphoreType.DMA((2,)),
            pltpu.SemaphoreType.DMA((2, window)),
            pltpu.SemaphoreType.DMA((2,)),
            pltpu.SemaphoreType.DMA((2, devices)),
            pltpu.SemaphoreType.DMA((2, 2, devices)),
            pltpu.SemaphoreType.DMA((3, devices)),
            pltpu.SemaphoreType.DMA((5, devices)),
        ],
        compiler_params=pltpu.CompilerParams(
            collective_id=0, has_side_effects=True, vmem_limit_bytes=62 * MIB
        ),
    )(alpha_start, beta_in, left_factor, right_factor, rows)
    per_call = 4
    rows_all = window * seqs
    factor = size * (size * size / seqs)
    scale_spec = pl.BlockSpec((rows_all, LANES), lambda b: (0, 0))
    factor_spec = pl.BlockSpec((per_call, size, size), lambda b: (b, 0, 0))
    kept_spec = pl.BlockSpec((per_call, rows_all, size), lambda b: (b, 0, 0))
    count_left = pl.pallas_call(
        functools.partial(counts_kernel, factor),
        grid=(blocks // per_call,),
        out_shape=jax.ShapeDtypeStruct(left_factor.shape, bf16),
        in_specs=[scale_spec, scale_spec, factor_spec, kept_spec, kept_spec],
        out_specs=factor_spec,
        compiler_params=pltpu.CompilerParams(vmem_limit_bytes=60 * MIB),
    )(
        post.reshape(rows_all, LANES),
        mean.reshape(rows_all, LANES),
        left_factor,
        paths.reshape(blocks, rows_all, size),
        values.reshape(blocks, rows_all, size),
    )
    log_scales = jnp.log(totals[1:, :, 0])
    return count_left, beta_out, log_scales


def fused_fits(seqs, blocks, size):
    if blocks % 16 or LANES % blocks or size % LANES or seqs % 16:
        return False
    return seqs % (LANES // blocks) == 0


def on_device(tokens, alpha_start, beta_in, emission, left_factor, right_factor):
    blocks_dev, block_size, _ = left_factor.shape
    seq_count = alpha_start.shape[0]
    window = tokens.shape[0]
    vocab_size = emission.shape[0]
    states = block_size * block_size

    def emission_rows(step):
        picked = tokens[step][:, None] == lax.broadcasted_iota(
            jnp.int32, (seq_count, vocab_size), 1
        )
        rows = jnp.dot(picked.astype(jnp.bfloat16), emission, preferred_element_type=jnp.float32)
        return rows[None, :, :]

    def path_sums(message):
        return jnp.einsum(
            "rns,rsp->rnp", message, right_factor, preferred_element_type=jnp.float32
        ).astype(jnp.bfloat16)

    forward_msg = jnp.transpose(alpha_start.reshape(seq_count, blocks_dev, block_size), (1, 0, 2))
    forwards = [forward_msg]
    received = []
    log_rows = []
    for step in range(1, window):
        arrived = lax.all_to_all(
            path_sums(forward_msg), "blk", split_axis=2, concat_axis=0, tiled=True
        )
        turned_paths = jnp.transpose(arrived, (2, 1, 0))
        received.append(turned_paths)
        ahead = jnp.einsum(
            "pnr,prq->pnq", turned_paths, left_factor, preferred_element_type=jnp.float32
        )
        weighted = ahead * emission_rows(step - 1)
        forward_total = lax.psum(jnp.sum(weighted, axis=(0, 2)), "blk")
        log_rows.append(jnp.log(forward_total / states))
        forward_msg = (states * weighted / forward_total[None, :, None]).astype(jnp.bfloat16)
        forwards.append(forward_msg)
    last_send = path_sums(forward_msg)
    received.append(
        jnp.transpose(
            lax.all_to_all(last_send, "blk", split_axis=2, concat_axis=0, tiled=True), (2, 1, 0)
        )
    )
    backward_msg = jnp.transpose(beta_in.reshape(seq_count, blocks_dev, block_size), (1, 0, 2))
    weights = []
    values = []
    for step in range(window, 0, -1):
        emitted = (emission_rows(step - 1) * backward_msg).astype(jnp.bfloat16)
        back_sums = jnp.einsum(
            "pnq,prq->pnr", emitted, left_factor, preferred_element_type=jnp.float32
        ).astype(jnp.bfloat16)
        if step == window:
            turned = lax.all_to_all(back_sums, "blk", split_axis=2, concat_axis=0, tiled=True)
        else:
            turned = lax.all_to_all(back_sums, "blk", split_axis=2, concat_axis=0, tiled=True)
        turned_back = jnp.transpose(turned, (2, 1, 0))
        prior = jnp.einsum(
            "rnp,rsp->rns", turned_back, right_factor, preferred_element_type=jnp.float32
        )
        norm_total, posterior_total = lax.psum(
            (jnp.sum(prior, axis=(0, 2)), jnp.sum(forwards[step - 1] * prior, axis=(0, 2))), "blk"
        )
        weights.append(
            (received[step - 1].astype(jnp.float32) / posterior_total[None, :, None]).astype(
                jnp.bfloat16
            )
        )
        values.append(emitted)
        backward_msg = (states * prior / norm_total[None, :, None]).astype(jnp.bfloat16)
    stacked_weights = jnp.concatenate(weights, axis=1)
    stacked_values = jnp.concatenate(values, axis=1)
    tally = jnp.einsum(
        "pnr,pnq->prq", stacked_weights, stacked_values, preferred_element_type=jnp.float32
    )
    count_left = (left_factor * tally * (block_size * states / seq_count)).astype(jnp.bfloat16)
    log_scales = jnp.stack(log_rows, axis=0)
    beta_out = jnp.transpose(backward_msg, (1, 0, 2)).reshape(seq_count, blocks_dev * block_size)
    return (count_left, beta_out, log_scales)


def solution(mesh):
    in_specs = (
        P(None, "groups"),
        P("groups", "blk"),
        P("groups", "blk"),
        P(),
        P("blk", None, None),
        P("blk", None, None),
    )
    out_specs = (P(("groups", "blk"), None, None), P("groups", "blk"), P(None, "groups"))
    devices = mesh.shape["blk"]

    def body(*operands):
        if fused_fits(operands[1].shape[0], *operands[4].shape[:2]):
            return on_device_fused(devices, *operands)
        return on_device(*operands)

    return jax.shard_map(
        body, mesh=mesh, in_specs=in_specs, out_specs=out_specs, check_vma=False
    )
```
